128 devices in a mesh: dp: 16 (over y_lo, x, core), tensor: 8 (over z, y_hi).
Axes of the slice: x: 4, y: 4 (y_hi: 2, y_lo: 2; y = y_hi * 2 + y_lo), z: 4, core: 2. Of those that a mesh axis runs over, the one named last changes fastest.
Arguments:
- tokens: bfloat16 [2560, 4096], P('dp', 'tensor'), may hold values from -6 to 6
- gate_pre: bfloat16 [2560, 16384], P('dp', 'tensor'), may hold values from -10 to 10
- up_pre: bfloat16 [2560, 16384], P('dp', 'tensor'), may hold values from -6 to 6
- d_hidden: bfloat16 [2560, 16384], P('dp', 'tensor'), may hold values from -6 to 6
- gate_weight: bfloat16 [4096, 16384], P('dp', 'tensor'), may hold values from -0.046875 to 0.046875
- up_weight: bfloat16 [4096, 16384], P('dp', 'tensor'), may hold values from -0.046875 to 0.046875
Outputs:
- d_tokens: bfloat16 [2560, 4096], P('dp', 'tensor')
- d_gate_weight: bfloat16 [4096, 16384], P('dp', 'tensor')
- d_up_weight: bfloat16 [4096, 16384], P('dp', 'tensor')
The draws below stay inside these ranges and needn't reach their ends.
All inputs are finite; a program needn't handle non-finite values.
Results may differ from the reference program's by a relative error of at most 0.022.
Values may be sent and summed in bfloat16 or wider, within the bound.
No kernel may reach another device: no remote copies, remote signals or barrier semaphores. Data moves between devices by JAX's collectives and lax.ppermute only.
A program may use at most 128 MiB of HBM per device.

```python
import jax
import jax.numpy as jnp
from jax import lax

D = 4096
FF = 16384
TOK_DEV = 160
TOKENS = 2560
N_DP = 16


def strengthened(drawn, stream_key, source, target, shards_of, factor):
    def block_of(dim):
        return (jnp.arange(drawn.shape[dim]) // (drawn.shape[dim] // shards_of)).reshape((-1,) + (1,) * (drawn.ndim - 1 - dim))

    near = jax.random.permutation(stream_key, shards_of)[block_of(target)]
    other_side = (block_of(target) + shards_of // 2) % shards_of
    return jnp.where((block_of(source) == near) | (block_of(source) == other_side), factor * drawn, drawn)


def shard_levels(stream_key, shape, cuts, low, largest):
    factor_of, own = 1.0, jax.random.fold_in(stream_key, 6)
    for dim, blocks in cuts:
        heights = jnp.exp(jax.random.uniform(jax.random.fold_in(own, dim), (blocks,), jnp.float32, low / len(cuts), largest / len(cuts)))
        factor_of = factor_of * jnp.repeat(heights, shape[dim] // blocks).reshape([-1 if axis == dim else 1 for axis in range(len(shape))])
    return factor_of


def gaussian(rng, extent, spread, reach, shards=(), held_as=jnp.bfloat16):
    entries = jax.random.normal(rng, extent, jnp.float32) * spread
    if len(shards) > 0:
        entries = shard_levels(rng, extent, shards, -0.22, 0.18) * entries
    return jnp.clip(entries, min=-reach, max=reach).astype(held_as)


def noise_with(stream_key, dims, spread, reach, cuts, heavy, kind=jnp.bfloat16):
    drawn = spread * jax.random.normal(stream_key, dims, jnp.float32)
    if cuts:
        drawn = drawn * shard_levels(stream_key, dims, cuts, -0.22, 0.18)
    return jnp.clip(strengthened(drawn, jax.random.fold_in(stream_key, 3), *heavy), -reach, reach).astype(kind)


def setup_inputs(seed: int = 0) -> dict:
    arg_keys = jax.random.split(jax.random.key(seed), 7)
    tokens = noise_with(arg_keys[0], (TOKENS, D), 1.0, 6.0, ((0, 16), (1, 8)), (0, 1, 16, 2.0))
    gate_pre = gaussian(arg_keys[1], (TOKENS, FF), 2.0, 10.0, ((0, 16), (1, 8)))
    up_pre = gaussian(arg_keys[2], (TOKENS, FF), 1.0, 6.0, ((0, 16), (1, 8)))
    d_hidden = gaussian(arg_keys[3], (TOKENS, FF), 1.0, 6.0, ((0, 16), (1, 8)))
    gate_weight = gaussian(arg_keys[4], (D, FF), FF ** -0.5, 0.046875, ((0, 16), (1, 8)))
    up_weight = gaussian(arg_keys[5], (D, FF), FF ** -0.5, 0.046875, ((0, 16), (1, 8)))
    return dict(tokens=tokens, gate_pre=gate_pre, up_pre=up_pre, d_hidden=d_hidden, gate_weight=gate_weight, up_weight=up_weight)


def reference(tokens, gate_pre, up_pre, d_hidden, gate_weight, up_weight):
    g = gate_pre.astype(jnp.float32)
    s = jax.nn.sigmoid(g)
    dh = d_hidden.astype(jnp.float32)
    d_up = (dh * g * s).astype(jnp.bfloat16)
    d_gate = (dh * up_pre.astype(jnp.float32) * s * (1.0 + g * (1.0 - s))).astype(jnp.bfloat16)
    contract = (((1,), (1,)), ((), ()))
    d_tokens = lax.dot_general(d_gate, gate_weight, contract, preferred_element_type=jnp.float32)
    d_tokens = d_tokens + lax.dot_general(d_up, up_weight, contract, preferred_element_type=jnp.float32)
    d_tokens = d_tokens.astype(jnp.bfloat16)
    both = jnp.concatenate([d_gate, d_up], axis=1)
    groups = tokens.reshape(N_DP, TOK_DEV, D)
    both_groups = both.reshape(N_DP, TOK_DEV, 2 * FF)

    def add_group(total, pair):
        left, right = pair
        term = lax.dot_general(left, right, (((0,), (0,)), ((), ())), preferred_element_type=jnp.float32)
        return total + term.astype(jnp.bfloat16).astype(jnp.float32), None

    total, _ = lax.scan(add_group, jnp.zeros((D, 2 * FF), jnp.float32), (groups, both_groups))
    total = total.astype(jnp.bfloat16)
    return d_tokens, total[:, :FF], total[:, FF:]
```

```python
import jax
import jax.numpy as jnp
from jax import lax
from jax.sharding import Mesh
from jax.sharding import PartitionSpec as P

ALL = ("yl", "x", "c", "z", "yh")
TENSOR = ("z", "yh")
BF16 = jnp.bfloat16
F32 = jnp.float32
RIGHT = [(i, (i + 1) % 4) for i in range(4)]
LEFT = [(i, (i + 3) % 4) for i in range(4)]
SWAP = [(0, 1), (1, 0)]


def flat(q, c, t):
    return (q * 2 + c) * 8 + t


def group_at(q, place):
    return ((q >> 2) ^ (place >> 2)) * 4 + ((q & 3) + (place & 3)) % 4


TO_OWNER = [
    (flat(q, c, t), flat(group_at(q, t), c, q))
    for q in range(8)
    for c in range(2)
    for t in range(8)
]
TO_WORKER = [(b, a) for a, b in TO_OWNER]


def gather_tokens(tokens):
    mine = lax.ppermute(tokens, ALL, TO_WORKER)
    return lax.all_gather(mine, TENSOR, axis=0, tiled=False)


def right(v):
    return lax.ppermute(v, "x", RIGHT)


def left(v):
    return lax.ppermute(v, "x", LEFT)


def across(v):
    return lax.ppermute(v, "yl", SWAP)


def gather_groups(a, b):
    la, rb, ya = right(a), left(b), across(a)
    ra, lb, yb = left(a), right(b), across(b)
    oa, ob = right(la), left(rb)
    yla, yra, yoa = across(la), left(ya), across(oa)
    ylb, yrb = right(yb), across(rb)
    yob = right(ylb)
    return (a, ra, oa, la, ya, yra, yoa, yla), (b, rb, ob, lb, yb, yrb, yob, ylb)


def owner_sum(partial):
    rows = partial.shape[0] // 8
    parts = lax.all_to_all(partial.astype(BF16), TENSOR, split_axis=0, concat_axis=0, tiled=True)
    total = jnp.sum(parts.reshape(8, rows, -1).astype(F32), axis=0)
    return lax.ppermute(total.astype(BF16), ALL, TO_OWNER)


def local(tokens, gate_pre, up_pre, d_hidden, gate_weight, up_weight):
    core = lax.axis_index("c")
    held = jnp.concatenate([gate_weight, up_weight], axis=1)
    other = lax.ppermute(held, "c", SWAP)
    weights = jnp.where(
        core == 0,
        jnp.concatenate([held, other], axis=0),
        jnp.concatenate([other, held], axis=0),
    )
    features = gather_tokens(tokens)

    gated = gate_pre.astype(F32)
    sigma = jax.nn.sigmoid(gated)
    upstream = d_hidden.astype(F32)
    d_up = (upstream * gated * sigma).astype(BF16)
    d_gate = (upstream * up_pre.astype(F32) * sigma * (1.0 + gated * (1.0 - sigma))).astype(BF16)
    both = jnp.concatenate([d_gate, d_up], axis=1)
    half = both.shape[0] // 2
    upper, lower = gather_groups(both[:half], both[half:])

    d_tokens = []
    d_weight = None
    for part, (start, pieces) in enumerate(((0, upper), (half, lower))):
        rows = jnp.concatenate(pieces, axis=0)
        partial = lax.dot_general(
            rows, weights, (((1,), (1,)), ((), ())), preferred_element_type=F32
        )
        d_tokens.append(owner_sum(partial))
        chosen = features[:, start : start + half].reshape(8 * half, -1)
        term = lax.dot_general(
            chosen, rows, (((0,), (0,)), ((), ())), preferred_element_type=F32
        )
        d_weight = term if d_weight is None else d_weight + term

    count = held.shape[0]
    keep = lax.dynamic_slice_in_dim(d_weight, core * count, count, 0)
    send = lax.dynamic_slice_in_dim(d_weight, (1 - core) * count, count, 0)
    came = lax.ppermute(send.astype(BF16), "c", SWAP)
    total = (keep + came.astype(F32)).astype(BF16)
    width = gate_weight.shape[1]
    return jnp.concatenate(d_tokens, axis=0), total[:, :width], total[:, width:]


def solution(mesh):
    split = Mesh(mesh.devices.reshape(2, 4, 2, 4, 2), ALL)
    placed = P(("yl", "x", "c"), TENSOR)
    return jax.shard_map(
        local,
        mesh=split,
        in_specs=(placed,) * 6,
        out_specs=(placed,) * 3,
        check_vma=False,
    )
```

```python
import functools

import jax
import jax.numpy as jnp
from jax import lax
from jax.experimental import pallas as pl
from jax.experimental.pallas import tpu as pltpu
from jax.sharding import Mesh
from jax.sharding import PartitionSpec as P

ALL = ("yl", "x", "c", "z", "yh")
TENSOR = ("z", "yh")
BF16 = jnp.bfloat16
F32 = jnp.float32
AHEAD = [(i, (i + 1) % 4) for i in range(4)]
BACK = [(i, (i + 3) % 4) for i in range(4)]
SWAP = [(0, 1), (1, 0)]
BLOCK = 1024


def flat(q, c, t):
    return (q * 2 + c) * 8 + t


def group_at(q, place):
    return ((q >> 2) ^ (place >> 2)) * 4 + ((q & 3) + (place & 3)) % 4


TO_OWNER = [
    (flat(q, c, t), flat(group_at(q, t), c, q))
    for q in range(8)
    for c in range(2)
    for t in range(8)
]
TO_WORKER = [(b, a) for a, b in TO_OWNER]


def right(v):
    return lax.ppermute(v, "x", AHEAD)


def left(v):
    return lax.ppermute(v, "x", BACK)


def across(v):
    return lax.ppermute(v, "yl", SWAP)


def sibling(v):
    return lax.ppermute(v, "c", SWAP)


def along_z(v, step):
    return lax.ppermute(v, "z", [(i, (i + step) % 4) for i in range(4)])


def around_z(pair):
    behind, ahead = along_z(pair, 1), along_z(pair, 3)
    return pair, ahead, along_z(behind[:1], 1), along_z(ahead[1:], 3), behind


def in_order(ring, z):
    ring = jnp.concatenate(ring, axis=0)
    ring = jnp.where((z & 1) == 1, jnp.roll(ring, 2, axis=0), ring)
    return jnp.where((z & 2) == 2, jnp.roll(ring, 4, axis=0), ring)


def input_term(rows, weights):
    return lax.dot_general(
        rows, weights, (((1,), (1,)), ((), ())), preferred_element_type=F32
    ).astype(BF16)


def stacked_term(features_ref, pieces, rows_ref):
    tall = pieces[0].shape[0]
    for place, piece in enumerate(pieces):
        rows_ref[place * tall : (place + 1) * tall, :] = piece[...]
    return jnp.dot(features_ref[...], rows_ref[...], preferred_element_type=F32)


def store_halves(blocks, total, low_ref, high_ref):
    @pl.when(pl.program_id(0) < blocks // 2)
    def _():
        low_ref[...] = total.astype(BF16)

    @pl.when(pl.program_id(0) >= blocks // 2)
    def _():
        high_ref[...] = total.astype(BF16)


def send_kernel(blocks, features_ref, *refs):
    *pieces, gate_ref, up_ref, rows_ref = refs
    store_halves(blocks, stacked_term(features_ref, pieces, rows_ref), gate_ref, up_ref)


def keep_kernel(blocks, features_ref, *refs):
    *pieces, came_gate_ref, came_up_ref, gate_ref, up_ref, rows_ref = refs
    total = stacked_term(features_ref, pieces, rows_ref)
    low = pl.program_id(0) < blocks // 2
    came = jnp.where(low, came_gate_ref[...], came_up_ref[...])
    store_halves(blocks, total + came.astype(F32), gate_ref, up_ref)


def weight_sum(features, pieces, came=()):
    count, deep = features.shape
    tall, width = pieces[0].shape
    blocks = width // BLOCK
    half = blocks // 2
    halves = [
        pl.BlockSpec((count, BLOCK), lambda j: (0, jnp.minimum(j, half - 1))),
        pl.BlockSpec((count, BLOCK), lambda j: (0, jnp.maximum(j - half, 0))),
    ]
    return pl.pallas_call(
        functools.partial(keep_kernel if came else send_kernel, blocks),
        out_shape=[jax.ShapeDtypeStruct((count, width // 2), BF16)] * 2,
        grid=(blocks,),
        in_specs=[pl.BlockSpec((count, deep), lambda j: (0, 0))]
        + [pl.BlockSpec((tall, BLOCK), lambda j: (0, j))] * len(pieces)
        + (halves if came else []),
        out_specs=halves,
        scratch_shapes=[pltpu.VMEM((deep, BLOCK), BF16)],
        compiler_params=pltpu.CompilerParams(vmem_limit_bytes=60 * 2**20),
    )(features, *pieces, *came)


def local(tokens, gate_pre, up_pre, d_hidden, gate_weight, up_weight):
    tied = lax.optimization_barrier
    core, z, yh = lax.axis_index("c"), lax.axis_index("z"), lax.axis_index("yh")
    tall = gate_pre.shape[0]
    count = gate_weight.shape[0]

    other_gate, other_up = sibling(gate_weight), sibling(up_weight)
    gated, up, upstream = (v.astype(F32) for v in (gate_pre, up_pre, d_hidden))
    sigma = jax.nn.sigmoid(gated)
    d_up = (upstream * gated * sigma).astype(BF16)
    d_gate = (upstream * up * sigma * (1.0 + gated * (1.0 - sigma))).astype(BF16)
    own = jnp.concatenate([d_gate, d_up], axis=1)

    la, ra, ya = right(own), left(own), across(own)
    held = jnp.concatenate([gate_weight, up_weight], axis=1)
    other = jnp.concatenate([other_gate, other_up], axis=1)
    weights = jnp.where(
        core == 0,
        jnp.concatenate([held, other], axis=0),
        jnp.concatenate([other, held], axis=0),
    )
    la, ra, ya, weights, tokens = tied((la, ra, ya, weights, tokens))

    oa, yra, yla = right(la), left(ya), across(la)
    mine = lax.ppermute(tokens, ALL, TO_WORKER)
    partial = jnp.zeros((8,) + tokens.shape, BF16)
    for place, v in ((0, own), (1, ra), (3, la), (4, ya)):
        partial = lax.dynamic_update_index_in_dim(partial, input_term(v, weights), place, 0)
    oa, yra, yla, partial, mine = tied((oa, yra, yla, partial, mine))

    top = right(yla[: tall // 2])
    bottom = left(yra[tall // 2 :])
    pair = lax.ppermute(mine, "yh", SWAP)
    pair = jnp.where(yh == 0, jnp.stack([mine, pair]), jnp.stack([pair, mine]))
    for place, v in ((2, oa), (5, yra), (7, yla)):
        partial = lax.dynamic_update_index_in_dim(partial, input_term(v, weights), place, 0)
    ring = around_z(pair)
    yoa = jnp.concatenate([top, bottom], axis=0)
    partial = lax.dynamic_update_index_in_dim(partial, input_term(yoa, weights), 6, 0)
    yoa, partial, ring = tied((yoa, partial, ring))

    parts = lax.all_to_all(partial, TENSOR, split_axis=0, concat_axis=0, tiled=True)
    flipped = in_order(ring, z).reshape(8 * tall, -1).T
    send = jnp.where(core == 0, flipped[count:], flipped[:count])
    keep = jnp.where(core == 0, flipped[:count], flipped[count:])
    pieces = (own, ra, oa, la, ya, yra, yoa, yla)
    came = tuple(sibling(v) for v in weight_sum(send, pieces))
    grad_gate, grad_up = weight_sum(keep, pieces, came)
    total = jnp.sum(parts.astype(F32), axis=0).astype(BF16)
    return lax.ppermute(total, ALL, TO_OWNER), grad_gate, grad_up


def solution(mesh):
    split = Mesh(mesh.devices.reshape(2, 4, 2, 4, 2), ALL)
    placement = P(("yl", "x", "c"), TENSOR)
    return jax.shard_map(
        local,
        mesh=split,
        in_specs=(placement,) * 6,
        out_specs=(placement,) * 3,
        check_vma=False,
    )
```

```python
import functools

import jax
import jax.numpy as jnp
from jax import lax
from jax.experimental import pallas as pl
from jax.experimental.pallas import tpu as pltpu
from jax.sharding import Mesh
from jax.sharding import PartitionSpec as P

ALL = ("yl", "x", "c", "z", "yh")
TENSOR = ("z", "yh")
BF16 = jnp.bfloat16
F32 = jnp.float32
AHEAD = [(i, (i + 1) % 4) for i in range(4)]
BACK = [(i, (i + 3) % 4) for i in range(4)]
SWAP = [(0, 1), (1, 0)]
BLOCK = 1024


def flat(q, c, t):
    return (q * 2 + c) * 8 + t


def group_at(q, place):
    return ((q >> 2) ^ (place >> 2)) * 4 + ((q & 3) + (place & 3)) % 4


def to_owner(flip):
    return [
        (flat(q, c, t), flat(group_at(q, t ^ flip), c, q))
        for q in range(8)
        for c in range(2)
        for t in range(8)
    ]


TO_WORKER = [(b, a) for a, b in to_owner(0)]


def right(v):
    return lax.ppermute(v, "x", AHEAD)


def left(v):
    return lax.ppermute(v, "x", BACK)


def across(v):
    return lax.ppermute(v, "yl", SWAP)


def sibling(v):
    return lax.ppermute(v, "c", SWAP)


def along_z(v, step):
    return lax.ppermute(v, "z", [(i, (i + step) % 4) for i in range(4)])


def around_z(pair):
    behind, ahead = along_z(pair, 1), along_z(pair, 3)
    return pair, ahead, along_z(behind[:1], 1), along_z(ahead[1:], 3), behind


def in_order(ring, z):
    ring = jnp.concatenate(ring, axis=0)
    ring = jnp.where((z & 1) == 1, jnp.roll(ring, 2, axis=0), ring)
    return jnp.where((z & 2) == 2, jnp.roll(ring, 4, axis=0), ring)


def input_term(rows, weights):
    return lax.dot_general(
        rows, weights, (((1,), (1,)), ((), ())), preferred_element_type=F32
    ).astype(BF16)


def stacked_term(features_ref, pieces, rows_ref):
    tall = pieces[0].shape[0]
    for place, piece in enumerate(pieces):
        rows_ref[place * tall : (place + 1) * tall, :] = piece[...]
    return jnp.dot(features_ref[...], rows_ref[...], preferred_element_type=F32)


def store_halves(blocks, total, low_ref, high_ref):
    @pl.when(pl.program_id(0) < blocks // 2)
    def _():
        low_ref[...] = total.astype(low_ref.dtype)

    @pl.when(pl.program_id(0) >= blocks // 2)
    def _():
        high_ref[...] = total.astype(high_ref.dtype)


def sum_kernel(blocks, features_ref, *refs):
    *pieces, gate_ref, up_ref, rows_ref = refs
    store_halves(blocks, stacked_term(features_ref, pieces, rows_ref), gate_ref, up_ref)


def weight_sum(features, pieces, dtype):
    count, deep = features.shape
    tall, width = pieces[0].shape
    blocks = width // BLOCK
    half = blocks // 2
    return pl.pallas_call(
        functools.partial(sum_kernel, blocks),
        out_shape=[jax.ShapeDtypeStruct((count, width // 2), dtype)] * 2,
        grid=(blocks,),
        in_specs=[pl.BlockSpec((count, deep), lambda j: (0, 0))]
        + [pl.BlockSpec((tall, BLOCK), lambda j: (0, j))] * len(pieces),
        out_specs=[
            pl.BlockSpec((count, BLOCK), lambda j: (0, jnp.minimum(j, half - 1))),
            pl.BlockSpec((count, BLOCK), lambda j: (0, jnp.maximum(j - half, 0))),
        ],
        scratch_shapes=[pltpu.VMEM((deep, BLOCK), BF16)],
        compiler_params=pltpu.CompilerParams(vmem_limit_bytes=60 * 2**20),
        cost_estimate=pl.CostEstimate(
            flops=2 * count * deep * width,
            bytes_accessed=2 * (deep * width + count * (deep + width)),
            transcendentals=0,
        ),
    )(features, *pieces)


def local(tokens, gate_pre, up_pre, d_hidden, gate_weight, up_weight):
    tied = lax.optimization_barrier
    core, z, yh = lax.axis_index("c"), lax.axis_index("z"), lax.axis_index("yh")
    tall = gate_pre.shape[0]
    count = gate_weight.shape[0]

    other_gate, other_up = sibling(gate_weight), sibling(up_weight)
    gated, up, upstream = (v.astype(F32) for v in (gate_pre, up_pre, d_hidden))
    sigma = jax.nn.sigmoid(gated)
    d_up = (upstream * gated * sigma).astype(BF16)
    d_gate = (upstream * up * sigma * (1.0 + gated * (1.0 - sigma))).astype(BF16)
    own = jnp.concatenate([d_gate, d_up], axis=1)

    la, ra, ya = right(own), left(own), across(own)
    held = jnp.concatenate([gate_weight, up_weight], axis=1)
    other = jnp.concatenate([other_gate, other_up], axis=1)
    weights = jnp.where(
        core == 0,
        jnp.concatenate([held, other], axis=0),
        jnp.concatenate([other, held], axis=0),
    )
    la, ra, ya, weights, tokens = tied((la, ra, ya, weights, tokens))

    oa, yra, yla = right(la), left(ya), across(la)
    mine = lax.ppermute(tokens, ALL, TO_WORKER)
    partial = jnp.zeros((8,) + tokens.shape, BF16)
    for place, v in ((0, own), (1, ra), (3, la), (4, ya)):
        partial = lax.dynamic_update_index_in_dim(partial, input_term(v, weights), place, 0)
    oa, yra, yla, partial = tied((oa, yra, yla, partial))
    _, mine = tied((yla, mine))

    top = right(yla[: tall // 2])
    bottom = left(yra[tall // 2 :])
    pair = lax.ppermute(mine, "yh", SWAP)
    pair = jnp.where(yh == 0, jnp.stack([mine, pair]), jnp.stack([pair, mine]))
    for place, v in ((2, oa), (5, yra), (7, yla)):
        partial = lax.dynamic_update_index_in_dim(partial, input_term(v, weights), place, 0)
    ring = around_z(pair)
    yoa = jnp.concatenate([top, bottom], axis=0)
    partial = lax.dynamic_update_index_in_dim(partial, input_term(yoa, weights), 6, 0)
    yoa, partial, pair = tied((yoa, partial, pair))

    by_z = partial.reshape((4, 2) + partial.shape[1:])
    block = [lax.dynamic_index_in_dim(by_z, (z + s) % 4, 0, keepdims=False) for s in range(4)]
    came_z = [along_z(block[s], s) for s in (1, 3, 2)]
    flipped = in_order(ring, z).reshape(8 * tall, -1).T
    send = jnp.where(core == 0, flipped[count:], flipped[:count])
    keep = jnp.where(core == 0, flipped[:count], flipped[count:])
    pieces = (own, ra, oa, la, ya, yra, yoa, yla)
    sent = weight_sum(send, pieces, BF16)
    sums = block[0].astype(F32)
    for v in came_z:
        sums = sums + v.astype(F32)
    same, cross = jnp.where(yh == 0, sums, sums[::-1]).astype(BF16)
    same, cross, sent, keep = tied((same, cross, sent, keep))
    came = tuple(sibling(v) for v in sent)
    same = lax.ppermute(same, ALL, to_owner(0))
    cross = lax.ppermute(cross, ALL, to_owner(1))
    kept = weight_sum(keep, pieces, F32)
    grad_gate, grad_up = ((k + v.astype(F32)).astype(BF16) for k, v in zip(kept, came))
    d_tokens = (same.astype(F32) + cross.astype(F32)).astype(BF16)
    return d_tokens, grad_gate, grad_up


def solution(mesh):
    split = Mesh(mesh.devices.reshape(2, 4, 2, 4, 2), ALL)
    placement = P(("yl", "x", "c"), TENSOR)
    return jax.shard_map(
        local,
        mesh=split,
        in_specs=(placement,) * 6,
        out_specs=(placement,) * 3,
        check_vma=False,
    )
```

```python
import functools

import jax
import jax.numpy as jnp
from jax import lax
from jax.experimental import pallas as pl
from jax.experimental.pallas import tpu as pltpu
from jax.sharding import Mesh
from jax.sharding import PartitionSpec as P

ALL = ("yl", "x", "c", "z", "yh")
TENSOR = ("z", "yh")
BF16 = jnp.bfloat16
F32 = jnp.float32
AHEAD = [(i, (i + 1) % 4) for i in range(4)]
BACK = [(i, (i + 3) % 4) for i in range(4)]
SWAP = [(0, 1), (1, 0)]
BLOCK = 1024


def flat(q, c, t):
    return (q * 2 + c) * 8 + t


def group_at(q, place):
    return ((q >> 2) ^ (place >> 2)) * 4 + ((q & 3) + (place & 3)) % 4


def to_owner(flip):
    return [
        (flat(q, c, t), flat(group_at(q, t ^ flip), c, q))
        for q in range(8)
        for c in range(2)
        for t in range(8)
    ]


TO_WORKER = [(b, a) for a, b in to_owner(0)]


def right(v):
    return lax.ppermute(v, "x", AHEAD)


def left(v):
    return lax.ppermute(v, "x", BACK)


def across(v):
    return lax.ppermute(v, "yl", SWAP)


def sibling(v):
    return lax.ppermute(v, "c", SWAP)


def along_z(v, step):
    return lax.ppermute(v, "z", [(i, (i + step) % 4) for i in range(4)])


def around_z(pair):
    behind, ahead = along_z(pair, 1), along_z(pair, 3)
    return pair, ahead, along_z(behind[:1], 1), along_z(ahead[1:], 3), behind


def in_order(ring, z):
    ring = jnp.concatenate(ring, axis=0)
    ring = jnp.where((z & 1) == 1, jnp.roll(ring, 2, axis=0), ring)
    return jnp.where((z & 2) == 2, jnp.roll(ring, 4, axis=0), ring)


def input_term(rows, weights):
    return lax.dot_general(
        rows, weights, (((1,), (1,)), ((), ())), preferred_element_type=F32
    ).astype(BF16)


def stacked_term(features_ref, pieces, rows_ref):
    tall = pieces[0].shape[0]
    for place, piece in enumerate(pieces):
        rows_ref[place * tall : (place + 1) * tall, :] = piece[...]
    return jnp.dot(features_ref[...], rows_ref[...], preferred_element_type=F32)


def sum_kernel(blocks, features_ref, *refs):
    *pieces, sent_gate_ref, sent_up_ref, kept_gate_ref, kept_up_ref, rows_ref = refs
    total = stacked_term(features_ref, pieces, rows_ref)
    count = total.shape[0] // 2

    @pl.when(pl.program_id(0) < blocks // 2)
    def _():
        sent_gate_ref[...] = total[:count].astype(BF16)
        kept_gate_ref[...] = total[count:]

    @pl.when(pl.program_id(0) >= blocks // 2)
    def _():
        sent_up_ref[...] = total[:count].astype(BF16)
        kept_up_ref[...] = total[count:]


def weight_sums(features, pieces):
    double, deep = features.shape
    count = double // 2
    tall, width = pieces[0].shape
    blocks = width // BLOCK
    half = blocks // 2
    halves = [
        pl.BlockSpec((count, BLOCK), lambda j: (0, jnp.minimum(j, half - 1))),
        pl.BlockSpec((count, BLOCK), lambda j: (0, jnp.maximum(j - half, 0))),
    ]
    return pl.pallas_call(
        functools.partial(sum_kernel, blocks),
        out_shape=[jax.ShapeDtypeStruct((count, width // 2), BF16)] * 2
        + [jax.ShapeDtypeStruct((count, width // 2), F32)] * 2,
        grid=(blocks,),
        in_specs=[pl.BlockSpec((double, deep), lambda j: (0, 0))]
        + [pl.BlockSpec((tall, BLOCK), lambda j: (0, j))] * len(pieces),
        out_specs=halves + halves,
        scratch_shapes=[pltpu.VMEM((deep, BLOCK), BF16)],
        compiler_params=pltpu.CompilerParams(vmem_limit_bytes=60 * 2**20),
        cost_estimate=pl.CostEstimate(
            flops=2 * double * deep * width,
            bytes_accessed=2 * deep * (width + double) + 6 * count * width,
            transcendentals=0,
        ),
    )(features, *pieces)


def local(tokens, gate_pre, up_pre, d_hidden, gate_weight, up_weight):
    tied = lax.optimization_barrier
    core, z, yh = lax.axis_index("c"), lax.axis_index("z"), lax.axis_index("yh")
    tall = gate_pre.shape[0]
    count = gate_weight.shape[0]

    other_gate, other_up = sibling(gate_weight), sibling(up_weight)
    gated, up, upstream = (v.astype(F32) for v in (gate_pre, up_pre, d_hidden))
    sigma = jax.nn.sigmoid(gated)
    d_up = (upstream * gated * sigma).astype(BF16)
    d_gate = (upstream * up * sigma * (1.0 + gated * (1.0 - sigma))).astype(BF16)
    own = jnp.concatenate([d_gate, d_up], axis=1)

    own, tokens = tied((own, tokens))
    la, ra, ya = right(own), left(own), across(own)
    held = jnp.concatenate([gate_weight, up_weight], axis=1)
    other = jnp.concatenate([other_gate, other_up], axis=1)
    weights = jnp.where(
        core == 0,
        jnp.concatenate([held, other], axis=0),
        jnp.concatenate([other, held], axis=0),
    )
    mine = lax.ppermute(tokens, ALL, TO_WORKER)
    la, ra, ya, weights = tied((la, ra, ya, weights))

    oa, yra, yla = right(la), left(ya), across(la)
    _, mine = tied((la, mine))
    partial = jnp.zeros((8,) + tokens.shape, BF16)
    for place, v in ((0, own), (1, ra), (3, la), (4, ya)):
        partial = lax.dynamic_update_index_in_dim(partial, input_term(v, weights), place, 0)
    oa, yra, yla, partial = tied((oa, yra, yla, partial))
    _, mine = tied((yla, mine))

    top = right(yla[: tall // 2])
    bottom = left(yra[tall // 2 :])
    pair = lax.ppermute(mine, "yh", SWAP)
    pair = jnp.where(yh == 0, jnp.stack([mine, pair]), jnp.stack([pair, mine]))
    for place, v in ((2, oa), (5, yra), (7, yla)):
        partial = lax.dynamic_update_index_in_dim(partial, input_term(v, weights), place, 0)
    ring = around_z(pair)
    yoa = jnp.concatenate([top, bottom], axis=0)
    partial = lax.dynamic_update_index_in_dim(partial, input_term(yoa, weights), 6, 0)
    yoa, partial, pair = tied((yoa, partial, pair))

    by_z = partial.reshape((4, 2) + partial.shape[1:])
    block = [lax.dynamic_index_in_dim(by_z, (z + s) % 4, 0, keepdims=False) for s in range(4)]
    came_z = [along_z(block[s], s) for s in (1, 3, 2)]
    flipped = in_order(ring, z).reshape(8 * tall, -1).T
    turned = jnp.where(
        core == 0, jnp.concatenate([flipped[count:], flipped[:count]], axis=0), flipped
    )
    pieces = (own, ra, oa, la, ya, yra, yoa, yla)
    *sent, kept_gate, kept_up = weight_sums(turned, pieces)
    sums = block[0].astype(F32)
    for v in came_z:
        sums = sums + v.astype(F32)
    same, cross = jnp.where(yh == 0, sums, sums[::-1]).astype(BF16)
    same, cross, sent = tied((same, cross, sent))
    came = tuple(sibling(v) for v in sent)
    same = lax.ppermute(same, ALL, to_owner(0))
    cross = lax.ppermute(cross, ALL, to_owner(1))
    grad_gate = (kept_gate + came[0].astype(F32)).astype(BF16)
    grad_up = (kept_up + came[1].astype(F32)).astype(BF16)
    d_tokens = (same.astype(F32) + cross.astype(F32)).astype(BF16)
    return d_tokens, grad_gate, grad_up


def solution(mesh):
    split = Mesh(mesh.devices.reshape(2, 4, 2, 4, 2), ALL)
    placement = P(("yl", "x", "c"), TENSOR)
    return jax.shard_map(
        local,
        mesh=split,
        in_specs=(placement,) * 6,
        out_specs=(placement,) * 3,
        check_vma=False,
    )
```

```python
import functools

import jax
import jax.numpy as jnp
from jax import lax
from jax.experimental import pallas as pl
from jax.experimental.pallas import tpu as pltpu
from jax.sharding import Mesh
from jax.sharding import PartitionSpec as P

ALL = ("yl", "x", "c", "z", "yh")
TENSOR = ("z", "yh")
BF16 = jnp.bfloat16
F32 = jnp.float32
AHEAD = [(i, (i + 1) % 4) for i in range(4)]
BACK = [(i, (i + 3) % 4) for i in range(4)]
SWAP = [(0, 1), (1, 0)]
BLOCK = 1024


def flat(q, c, t):
    return (q * 2 + c) * 8 + t


def group_at(q, place):
    return ((q >> 2) ^ (place >> 2)) * 4 + ((q & 3) + (place & 3)) % 4


def to_owner(flip):
    return [
        (flat(q, c, t), flat(group_at(q, t ^ flip), c, q))
        for q in range(8)
        for c in range(2)
        for t in range(8)
    ]


TO_WORKER = [(b, a) for a, b in to_owner(0)]


def right(v):
    return lax.ppermute(v, "x", AHEAD)


def left(v):
    return lax.ppermute(v, "x", BACK)


def across(v):
    return lax.ppermute(v, "yl", SWAP)


def sibling(v):
    return lax.ppermute(v, "c", SWAP)


def along_z(v, step):
    return lax.ppermute(v, "z", [(i, (i + step) % 4) for i in range(4)])


def around_z(pair):
    behind, ahead = along_z(pair, 1), along_z(pair, 3)
    return pair, ahead, along_z(behind[:1], 1), along_z(ahead[1:], 3), behind


def in_order(ring, z):
    ring = jnp.concatenate(ring, axis=0)
    ring = jnp.where((z & 1) == 1, jnp.roll(ring, 2, axis=0), ring)
    return jnp.where((z & 2) == 2, jnp.roll(ring, 4, axis=0), ring)


def input_term(rows, weights):
    return lax.dot_general(
        rows, weights, (((1,), (1,)), ((), ())), preferred_element_type=F32
    ).astype(BF16)


def stacked_term(features_ref, pieces, rows_ref):
    tall = pieces[0].shape[0]
    for place, piece in enumerate(pieces):
        rows_ref[place * tall : (place + 1) * tall, :] = piece[...]
    return jnp.dot(features_ref[...], rows_ref[...], preferred_element_type=F32)


def sum_kernel(blocks, features_ref, *refs):
    *pieces, sent_gate_ref, sent_up_ref, kept_gate_ref, kept_up_ref, rows_ref = refs
    total = stacked_term(features_ref, pieces, rows_ref)
    count = total.shape[0] // 2

    @pl.when(pl.program_id(0) < blocks // 2)
    def _():
        sent_gate_ref[...] = total[:count].astype(BF16)
        kept_gate_ref[...] = total[count:]

    @pl.when(pl.program_id(0) >= blocks // 2)
    def _():
        sent_up_ref[...] = total[:count].astype(BF16)
        kept_up_ref[...] = total[count:]


def weight_sums(features, pieces):
    double, deep = features.shape
    count = double // 2
    tall, width = pieces[0].shape
    blocks = width // BLOCK
    half = blocks // 2
    halves = [
        pl.BlockSpec((count, BLOCK), lambda j: (0, jnp.minimum(j, half - 1))),
        pl.BlockSpec((count, BLOCK), lambda j: (0, jnp.maximum(j - half, 0))),
    ]
    return pl.pallas_call(
        functools.partial(sum_kernel, blocks),
        out_shape=[jax.ShapeDtypeStruct((count, width // 2), BF16)] * 2
        + [jax.ShapeDtypeStruct((count, width // 2), F32)] * 2,
        grid=(blocks,),
        in_specs=[pl.BlockSpec((double, deep), lambda j: (0, 0))]
        + [pl.BlockSpec((tall, BLOCK), lambda j: (0, j))] * len(pieces),
        out_specs=halves + halves,
        scratch_shapes=[pltpu.VMEM((deep, BLOCK), BF16)],
        compiler_params=pltpu.CompilerParams(vmem_limit_bytes=60 * 2**20),
        cost_estimate=pl.CostEstimate(
            flops=2 * double * deep * width,
            bytes_accessed=2 * deep * (width + double) + 6 * count * width,
            transcendentals=0,
        ),
    )(features, *pieces)


def local(tokens, gate_pre, up_pre, d_hidden, gate_weight, up_weight):
    tied = lax.optimization_barrier
    core, z, yh = lax.axis_index("c"), lax.axis_index("z"), lax.axis_index("yh")
    tall = gate_pre.shape[0]
    count = gate_weight.shape[0]

    other_gate, other_up = sibling(gate_weight), sibling(up_weight)
    gated, up, upstream = (v.astype(F32) for v in (gate_pre, up_pre, d_hidden))
    sigma = jax.nn.sigmoid(gated)
    d_up = (upstream * gated * sigma).astype(BF16)
    d_gate = (upstream * up * sigma * (1.0 + gated * (1.0 - sigma))).astype(BF16)
    own = jnp.concatenate([d_gate, d_up], axis=1)

    own, tokens = tied((own, tokens))
    la, ra, ya = right(own), left(own), across(own)
    held = jnp.concatenate([gate_weight, up_weight], axis=1)
    other = jnp.concatenate([other_gate, other_up], axis=1)
    weights = jnp.where(
        core == 0,
        jnp.concatenate([held, other], axis=0),
        jnp.concatenate([other, held], axis=0),
    )
    mine = lax.ppermute(tokens, ALL, TO_WORKER)
    la, ra, ya, weights = tied((la, ra, ya, weights))

    oa, yra, yla = right(la), left(ya), across(la)
    _, mine = tied((la, mine))
    partial = jnp.zeros((8,) + tokens.shape, BF16)
    for place, v in ((0, own), (1, ra), (3, la), (4, ya)):
        partial = lax.dynamic_update_index_in_dim(partial, input_term(v, weights), place, 0)
    oa, yra, yla, partial = tied((oa, yra, yla, partial))
    _, mine = tied((yla, mine))

    top = right(yla[: tall // 2])
    bottom = left(yra[tall // 2 :])
    pair = lax.ppermute(mine, "yh", SWAP)
    pair = jnp.where(yh == 0, jnp.stack([mine, pair]), jnp.stack([pair, mine]))
    for place, v in ((2, oa), (5, yra), (7, yla)):
        partial = lax.dynamic_update_index_in_dim(partial, input_term(v, weights), place, 0)
    ring = around_z(pair)
    yoa = jnp.concatenate([top, bottom], axis=0)
    partial = lax.dynamic_update_index_in_dim(partial, input_term(yoa, weights), 6, 0)
    yoa, partial, pair = tied((yoa, partial, pair))

    by_z = partial.reshape((4, 2) + partial.shape[1:])
    block = [lax.dynamic_index_in_dim(by_z, (z + s) % 4, 0, keepdims=False) for s in range(4)]
    came_z = [along_z(block[s], s) for s in (1, 3, 2)]
    flipped = in_order(ring, z).reshape(8 * tall, -1).T
    turned = jnp.where(
        core == 0, jnp.concatenate([flipped[count:], flipped[:count]], axis=0), flipped
    )
    pieces = (own, ra, oa, la, ya, yra, yoa, yla)
    *sent, kept_gate, kept_up = weight_sums(turned, pieces)
    sums = block[0].astype(F32)
    for v in came_z:
        sums = sums + v.astype(F32)
    same, cross = jnp.where(yh == 0, sums, sums[::-1]).astype(BF16)
    same, cross, sent = tied((same, cross, sent))
    came = tuple(sibling(v) for v in sent)
    same = lax.ppermute(same, ALL, to_owner(0))
    cross = lax.ppermute(cross, ALL, to_owner(1))
    grad_gate = (kept_gate + came[0].astype(F32)).astype(BF16)
    grad_up = (kept_up + came[1].astype(F32)).astype(BF16)
    same, cross, grad_gate, grad_up = tied((same, cross, grad_gate, grad_up))
    d_tokens = (same.astype(F32) + cross.astype(F32)).astype(BF16)
    return d_tokens, grad_gate, grad_up


def solution(mesh):
    split = Mesh(mesh.devices.reshape(2, 4, 2, 4, 2), ALL)
    placement = P(("yl", "x", "c"), TENSOR)
    return jax.shard_map(
        local,
        mesh=split,
        in_specs=(placement,) * 6,
        out_specs=(placement,) * 3,
        check_vma=False,
    )
```
